32 devices in a mesh: chan: 8 (over z, core), grp: 4 (over y, x).
Axes of the slice: x: 2, y: 2, z: 4, core: 2. Of those that a mesh axis runs over, the one named last changes fastest.
Arguments:
- residual: bfloat16 [128, 4096], P('grp', 'chan'), may hold values from -6 to 6
- conv_input: bfloat16 [128, 8192], P('grp', 'chan'), may hold values from -6 to 6
- gate_input: bfloat16 [128, 8192], P('grp', 'chan'), may hold values from -6 to 6
- conv_state: bfloat16 [128, 3, 8192], P('grp', None, 'chan'), may hold values from -6 to 6
- conv_weight: float32 [4, 8192], P(None, 'chan'), may hold values from -3 to 3
- conv_bias: float32 [8192], P('chan'), may hold values from -1 to 1
- state_proj: bfloat16 [8192, 288], P('chan'), may hold values from -0.0625 to 0.0625
- step_proj: bfloat16 [256, 8192], P(None, 'chan'), may hold values from -0.375 to 0.375
- step_bias: float32 [8192], P('chan'), may hold values from -5 to -1
- decay_rate: float32 [16, 8192], P(None, 'chan'), may hold values from 1 to 16
- skip_gain: float32 [8192], P('chan'), may hold values from 0.5 to 1.5
- ssm_state: float32 [128, 16, 8192], P('grp', None, 'chan'), may hold values from -6 to 6
- out_proj: bfloat16 [8192, 4096], P('chan'), may hold values from -0.0625 to 0.0625
- router: bfloat16 [4096, 4], P('chan'), may hold values from -0.09375 to 0.09375
- expert_ids: int32 [128, 2], P('grp'), may hold values from 0 to 3, all different within a row; in each aligned block of 32 rows (0 to 31, 32 to 63, ...) at most 24 rows name the same one
- expert_gate: bfloat16 [4, 4096, 16384], P('grp', None, 'chan'), may hold values from -0.09375 to 0.09375
- expert_up: bfloat16 [4, 4096, 16384], P('grp', None, 'chan'), may hold values from -0.09375 to 0.09375
- expert_down: bfloat16 [4, 16384, 4096], P('grp', 'chan'), may hold values from -0.046875 to 0.046875
Outputs:
- layer_out: bfloat16 [128, 4096], P('grp', 'chan')
- new_state: float32 [128, 16, 8192], P('grp', None, 'chan')
The draws below stay inside these ranges and needn't reach their ends.
Inputs may be any that keep to these rules, and one draw needn't show every extreme that they name: `expert_ids`: each request names two different experts; among the 32 requests of one group no expert is named more than 24 times, and in some group some expert is named exactly 24 times.
All inputs are finite; a program needn't handle non-finite values.
Results may differ from the reference program's by a relative error of at most 0.0056.
The reference program's roundings to bfloat16 on the way count: a program that leaves them out, or rounds other values in their place, can miss the bound.
Values may be sent and summed in bfloat16 or wider, within the bound.
A program may use at most 192 MiB of HBM per device.

```python
import math
import jax
import jax.numpy as jnp
import numpy as np
from jax import lax

D = 4096
CH = 8192
RANK = 256
NSTATE = 16
FF_E = 16384
EXPERTS = 4
REQ_DEV = 32
REQS = 128
SPLIT = 1
CAP = 24
N_GRP = 4


def block_levels(own_key, dims, cuts, least, largest):
    factor_of = 1.0
    for dim, blocks in cuts:
        steps = jax.random.uniform(jax.random.fold_in(jax.random.fold_in(own_key, 6), dim), (blocks,), jnp.float32, least / len(cuts), largest / len(cuts))
        factor_of = factor_of * jnp.repeat(jnp.exp(steps), dims[dim] // blocks).reshape((-1,) + (1,) * (len(dims) - 1 - dim))
    return factor_of


def routed_block(key, own, number, rows, number_of, top, bound, lean):
    order = jax.random.permutation(key, number_of)
    crowded, common = portions_of(number_of, rows * top, bound, lean, True), portions_of(number_of, rows * top, bound, lean, False)
    places = jnp.arange(number_of)

    def named(lengths, rotation):
        used = int((lengths > 0).sum())
        fixed = max(1, used // 4)
        shifted = fixed + (places - fixed + rotation * (used - fixed)) % max(1, number_of - fixed)
        return jnp.zeros((number_of,), jnp.int32).at[order[jnp.where(places < fixed, places, shifted)]].set(jnp.asarray(lengths, jnp.int32))

    lengths = jnp.where(number % 4 == 0, named(crowded, number // 4), named(common, number - number // 4 - 1))
    mixed = jax.random.permutation(jax.random.fold_in(own, 3), number_of)
    donor, taker = mixed[0:number_of // 2 * 2:2], mixed[1:number_of // 2 * 2:2]
    margin = jnp.minimum(lengths[donor] - 1, bound - lengths[taker]) // 2
    margin = jnp.where((donor == order[0]) | (taker == order[0]) | (lengths[taker] == 0), 0, jnp.maximum(margin, 0))
    shifted = jax.random.randint(jax.random.fold_in(own, 4), (number_of // 2,), 0, 1 << 20) % (margin + 1)
    lengths = lengths.at[donor].add(-shifted).at[taker].add(shifted)
    items = jnp.searchsorted(jnp.cumsum(lengths), jnp.arange(rows * top), side="right").astype(jnp.int32)
    grid = items.reshape(top, rows).T
    grid = grid[jax.random.permutation(jax.random.fold_in(own, 1), rows)]
    rotation = jax.random.randint(jax.random.fold_in(own, 2), (rows, 1), 0, top)
    return jnp.take_along_axis(grid, (jnp.arange(top)[None, :] + rotation) % top, axis=1)


def portions_of(amount, total, limit, skew, full):
    loads = [(1 << 20) // math.isqrt(rank ** skew) + 1 for rank in range(1, amount + 1)]
    largest = limit if full else min(limit, max(-(-total // amount), total * loads[0] // sum(loads)))
    least = 1 if total - largest >= amount - 1 else 0
    given, surplus = [largest] + [least] * (amount - 1), total - largest - least * (amount - 1)
    while surplus > 0:
        movable = [i for i in range(1, amount) if given[i] < largest] or [i for i in range(1, amount) if given[i] < limit]
        whole, left = sum([loads[i] for i in movable]), surplus
        for i in movable:
            extra = min(limit - given[i], max(1, left * loads[i] // whole), surplus)
            given[i] = given[i] + extra
            surplus = surplus - extra
    return np.array(given)


def bell_draw(key, dims, deviation, most, pieces=(), kind=jnp.bfloat16):
    array = jax.random.normal(key, dims, jnp.float32) * deviation
    if len(pieces) > 0:
        array = block_levels(key, dims, pieces, -0.22, 0.18) * array
    return jnp.clip(array, min=-most, max=most).astype(kind)


def setup_inputs(seed: int = 0) -> dict:
    arg_keys = jax.random.split(jax.random.key(seed), 19)
    residual = bell_draw(arg_keys[0], (REQS, D), 1.0, 6.0, ((0, 4), (1, 8)))
    conv_input = bell_draw(arg_keys[1], (REQS, CH), 1.0, 6.0, ((0, 4), (1, 8)))
    gate_input = bell_draw(arg_keys[2], (REQS, CH), 1.0, 6.0, ((0, 4), (1, 8)))
    conv_state = bell_draw(arg_keys[3], (REQS, 3, CH), 1.0, 6.0, ((0, 4), (2, 8)))
    conv_weight = bell_draw(arg_keys[4], (4, CH), 4 ** -0.5, 3.0, ((1, 8),), jnp.float32)
    conv_bias = jnp.clip(jax.random.uniform(arg_keys[5], (CH,), jnp.float32, -1.0, 1.0) * block_levels(arg_keys[5], (CH,), ((0, 8),), -0.4, 0.0), -1.0, 1.0)
    state_proj = bell_draw(arg_keys[6], (CH, RANK + 2 * NSTATE), CH ** -0.5, 0.0625, ((0, 8),))
    step_proj = bell_draw(arg_keys[7], (RANK, CH), RANK ** -0.5, 0.375, ((1, 8),))
    step_bias = jnp.clip(-5.0 + 4.0 * jax.random.uniform(arg_keys[8], (CH,), jnp.float32) ** block_levels(arg_keys[8], (CH,), ((0, 8),), -0.2, 0.2), -5.0, -1.0)
    decay_rate = jnp.clip(jnp.exp(math.log(16.0) - 2.7725887 * jax.random.uniform(arg_keys[9], (NSTATE, CH), jnp.float32) ** block_levels(arg_keys[9], (NSTATE, CH), ((1, 8),), -0.2, 0.2)), 1.0, 16.0)
    skip_gain = jnp.clip(0.5 + 1.0 * jax.random.uniform(arg_keys[10], (CH,), jnp.float32) ** block_levels(arg_keys[10], (CH,), ((0, 8),), -0.2, 0.2), 0.5, 1.5)
    ssm_state = bell_draw(arg_keys[11], (REQS, NSTATE, CH), 1.0, 6.0, ((0, 4), (2, 8)), jnp.float32)
    out_proj = bell_draw(arg_keys[12], (CH, D), CH ** -0.5, 0.0625, ((0, 8),))
    router = bell_draw(arg_keys[13], (D, EXPERTS), D ** -0.5, 0.09375, ((0, 8),))
    expert_ids_keys = jax.random.split(jax.random.fold_in(arg_keys[14], 1), REQS // REQ_DEV)
    expert_ids_turns = jax.random.permutation(jax.random.fold_in(arg_keys[14], 3), REQS // REQ_DEV)
    expert_ids = jax.vmap(lambda own, number: routed_block(jax.random.fold_in(arg_keys[14], 2), own, number, REQ_DEV, EXPERTS, 2, CAP, 2))(expert_ids_keys, expert_ids_turns).reshape((REQS, 2))
    expert_gate = bell_draw(arg_keys[15], (EXPERTS * SPLIT, D, FF_E // SPLIT), D ** -0.5, 0.09375, ((0, 4), (2, 8)))
    expert_up = bell_draw(arg_keys[16], (EXPERTS * SPLIT, D, FF_E // SPLIT), D ** -0.5, 0.09375, ((0, 4), (2, 8)))
    expert_down = bell_draw(arg_keys[17], (EXPERTS * SPLIT, FF_E // SPLIT, D), FF_E ** -0.5, 0.046875, ((0, 4), (1, 8)))
    return dict(residual=residual, conv_input=conv_input, gate_input=gate_input, conv_state=conv_state, conv_weight=conv_weight, conv_bias=conv_bias, state_proj=state_proj, step_proj=step_proj, step_bias=step_bias, decay_rate=decay_rate, skip_gain=skip_gain, ssm_state=ssm_state, out_proj=out_proj, router=router, expert_ids=expert_ids, expert_gate=expert_gate, expert_up=expert_up, expert_down=expert_down)


EPSILON = 1e-06

def reference(residual, conv_input, gate_input, conv_state, conv_weight, conv_bias, state_proj, step_proj, step_bias, decay_rate, skip_gain, ssm_state, out_proj, router, expert_ids, expert_gate, expert_up, expert_down):
    window = conv_state.astype(jnp.float32)
    convolved = conv_weight[0] * window[:, 0] + conv_weight[1] * window[:, 1] + conv_weight[2] * window[:, 2] + conv_weight[3] * conv_input.astype(jnp.float32) + conv_bias
    inner_act = jax.nn.silu(convolved).astype(jnp.bfloat16)
    projected = jnp.dot(inner_act, state_proj, preferred_element_type=jnp.float32)
    step_raw = projected[:, :RANK]
    input_mix = projected[:, RANK:RANK + NSTATE]
    output_mix = projected[:, RANK + NSTATE:]
    step_norm = (step_raw * lax.rsqrt(lax.optimization_barrier(jnp.mean(step_raw * step_raw, axis=1, keepdims=True)) + EPSILON)).astype(jnp.bfloat16)
    step_size = jax.nn.softplus(jnp.dot(step_norm, step_proj, preferred_element_type=jnp.float32) + step_bias)
    inner_wide = inner_act.astype(jnp.float32)
    decay_factor = jnp.exp(-step_size[:, None, :] * decay_rate[None, :, :])
    new_state = decay_factor * ssm_state + (step_size * inner_wide)[:, None, :] * input_mix[:, :, None]
    readout = lax.optimization_barrier(jnp.sum(output_mix[:, :, None] * new_state, axis=1)) + skip_gain * inner_wide
    gated_out = (readout * jax.nn.silu(gate_input.astype(jnp.float32))).astype(jnp.bfloat16)
    hidden_mid = residual.astype(jnp.float32) + jnp.dot(gated_out, out_proj, preferred_element_type=jnp.float32)
    inv_rms = lax.rsqrt(lax.optimization_barrier(jnp.mean(hidden_mid * hidden_mid, axis=1)) + EPSILON)
    normed = (hidden_mid * inv_rms[:, None]).astype(jnp.bfloat16)
    logits = jnp.dot(hidden_mid, router.astype(jnp.float32), precision=lax.Precision.HIGHEST) * inv_rms[:, None]
    labels = jnp.arange(EXPERTS, dtype=jnp.int32)
    chosen = lax.optimization_barrier(jnp.sum(logits[:, None, :] * (expert_ids[:, :, None] == labels).astype(jnp.float32), axis=2))
    weight_first = jax.nn.sigmoid(chosen[:, 0] - chosen[:, 1])
    weight_second = 1.0 - weight_first
    grouped = expert_ids.reshape(N_GRP, 2 * REQ_DEV)
    matches = (grouped[:, :, None] == labels).astype(jnp.int32)
    position = lax.optimization_barrier(jnp.sum((jnp.cumsum(matches, axis=1) - matches) * matches, axis=2))
    slot_index = (jnp.arange(N_GRP, dtype=jnp.int32)[:, None] * CAP + position).reshape(-1).astype(jnp.int32)
    flat_ids = expert_ids.reshape(-1).astype(jnp.int32)
    repeated = jnp.repeat(normed, 2, axis=0)

    def run_expert(expert_index):
        target = jnp.where(flat_ids == expert_index, slot_index, N_GRP * CAP).astype(jnp.int32)
        tile_rows = jnp.zeros((N_GRP * CAP, D), jnp.bfloat16).at[target].set(repeated, mode='drop')
        total = jnp.zeros((N_GRP * CAP, D), jnp.float32)
        for part_index in range(SPLIT):
            which = expert_index * SPLIT + part_index
            gate_sum = jnp.dot(tile_rows, expert_gate[which], preferred_element_type=jnp.float32)
            up_sum = jnp.dot(tile_rows, expert_up[which], preferred_element_type=jnp.float32)
            hidden = (jax.nn.silu(gate_sum) * up_sum).astype(jnp.bfloat16)
            piece = jnp.dot(hidden, expert_down[which], preferred_element_type=jnp.float32).astype(jnp.bfloat16)
            piece = lax.optimization_barrier(piece)
            total = total + piece.astype(jnp.float32)
        return total
    results = lax.map(run_expert, jnp.arange(EXPERTS, dtype=jnp.int32))
    answers = results[flat_ids, slot_index].reshape(REQS, 2, D)
    layer_out = (hidden_mid + weight_first[:, None] * answers[:, 0] + weight_second[:, None] * answers[:, 1]).astype(jnp.bfloat16)
    return (layer_out, new_state)
```

```python
import functools

import jax
import jax.numpy as jnp
from jax import lax
from jax.experimental import pallas as pl
from jax.experimental.pallas import tpu as pltpu
from jax.sharding import PartitionSpec as P

EPSILON = 1e-06
F32 = jnp.float32
BF16 = jnp.bfloat16


def fused(
    chans,
    groups,
    experts,
    inner_ref,
    residual_ref,
    gate_in_ref,
    state_proj_ref,
    step_proj_ref,
    step_bias_ref,
    decay_ref,
    skip_ref,
    router_ref,
    ids_ref,
    ssm_hbm,
    out_proj_hbm,
    gate_hbm,
    up_hbm,
    down_hbm,
    layer_ref,
    state_hbm,
    w_gate,
    w_up,
    w_down,
    w_share,
    state,
    partial,
    proj_send,
    proj_recv,
    proj_all,
    proj,
    step_buf,
    drive_buf,
    read_buf,
    mix_send,
    mix_recv,
    mid_send,
    mid_recv,
    rows_x,
    stat_own,
    stat_recv,
    stat_all,
    acc_gate,
    acc_up,
    hidden,
    pair_send,
    pair_recv,
    ans_send,
    ans_recv,
    fin_send,
    fin_recv,
    local_sem,
    send_sem,
    recv_sem,
):
    me = lax.axis_index("chan")
    grp = lax.axis_index("grp")
    core = lax.rem(me, 2)
    zed = lax.div(me, 2)
    zeds = chans // 2
    partner = me + 1 - 2 * core
    sharers = groups // experts
    rows, width = residual_ref.shape
    full = width * chans
    half = full // 2
    chn = inner_ref.shape[1]
    rank = step_proj_ref.shape[0]
    nst = decay_ref.shape[0]
    hid = w_down.shape[0]
    rn = rows // chans
    allrows = rows * groups

    counters = {"local": 0, "remote": 0}

    def local(src, dst):
        k = counters["local"]
        counters["local"] += 1
        copy = pltpu.make_async_copy(src, dst, local_sem.at[k])
        copy.start()
        return copy

    def remote(src, dst, **to):
        k = counters["remote"]
        counters["remote"] += 1
        copy = pltpu.make_async_remote_copy(
            src_ref=src,
            dst_ref=dst,
            send_sem=send_sem.at[k],
            recv_sem=recv_sem.at[k],
            device_id=to,
            device_id_type=pl.DeviceIdType.MESH,
        )
        copy.start()
        sent.append(copy)
        return copy

    sent = []

    def columns(z, other):
        parity = (1 - core) if other else core
        return pl.ds(pl.multiple_of((2 * z + parity) * width, width), width)

    state_in = local(ssm_hbm, state)
    mixer_in = [
        local(
            out_proj_hbm.at[:, columns(z, p == 0)],
            w_share.at[pl.ds(p * chn, chn), pl.ds(z * width, width)],
        )
        for p in range(2)
        for z in range(zeds)
    ]
    expert_in = [[], []]
    for p in range(2):
        for src, dst in ((gate_hbm, w_gate), (up_hbm, w_up)):
            for z in range(zeds):
                expert_in[p].append(
                    local(
                        src.at[0, columns(z, p == 1), :],
                        dst.at[p, pl.ds(z * width, width), :],
                    )
                )
    down_in = [
        local(down_hbm.at[0, :, columns(z, True)], w_down.at[:, pl.ds(z * width, width)])
        for z in range(zeds)
    ]

    barrier = pltpu.get_barrier_semaphore()
    for d in range(1, chans):
        pl.semaphore_signal(
            barrier,
            inc=1,
            device_id={"chan": lax.rem(me + d, chans)},
            device_id_type=pl.DeviceIdType.MESH,
        )
    for d in range(1, groups):
        pl.semaphore_signal(
            barrier,
            inc=1,
            device_id={"grp": lax.rem(grp + d, groups)},
            device_id_type=pl.DeviceIdType.MESH,
        )

    inner = inner_ref[...]
    padded = proj.shape[1]
    partial[:, rank:] = jnp.zeros((rows, padded - rank), F32)
    partial[:, : rank + 2 * nst] = jnp.dot(
        inner, state_proj_ref[...], preferred_element_type=F32
    )
    for j in range(chans):
        proj_send[j] = partial[j * rn : (j + 1) * rn, :]
    pl.semaphore_wait(barrier, chans - 1 + groups - 1)
    arrivals = []
    for d in range(1, chans):
        to = lax.rem(me + d, chans)
        arrivals.append(remote(proj_send.at[to], proj_recv.at[d], chan=to))
    total = proj_send[me]
    for d in range(1, chans):
        arrivals[d - 1].wait_recv()
        total = total + proj_recv[d]
    proj_all[me] = total
    arrivals = []
    for d in range(1, chans):
        to = lax.rem(me + d, chans)
        arrivals.append(remote(proj_all.at[me], proj_all.at[me], chan=to))
    inner_wide = inner.astype(F32)
    gate_in = gate_in_ref[...].astype(F32)
    for copy in arrivals:
        copy.wait_recv()
    for j in range(chans):
        proj[j * rn : (j + 1) * rn, :] = proj_all[j]

    step_raw = proj[:, :rank]
    step_norm = (
        step_raw * lax.rsqrt(jnp.mean(step_raw * step_raw, axis=1, keepdims=True) + EPSILON)
    ).astype(BF16)
    logit = jnp.dot(step_norm, step_proj_ref[...], preferred_element_type=F32) + step_bias_ref[...]
    step = jnp.maximum(logit, 0.0) + jnp.log1p(jnp.exp(-jnp.abs(logit)))
    step_buf[...] = step
    drive_buf[...] = step * inner_wide
    mixing = proj[:, rank:].T
    in_mix, out_mix = mixing[:nst], mixing[nst : 2 * nst]
    request = lax.broadcasted_iota(jnp.int32, (nst, rows), 1)
    state_in.wait()

    def update(r, carry):
        mine = request == r
        mix_in = jnp.sum(jnp.where(mine, in_mix, 0.0), axis=1, keepdims=True)
        mix_out = jnp.sum(jnp.where(mine, out_mix, 0.0), axis=1, keepdims=True)
        row = pl.ds(r, 1)
        new = jnp.exp(-step_buf[row, :] * decay_ref[...]) * state[r] + drive_buf[row, :] * mix_in
        state[r] = new
        read_buf[row, :] = jnp.sum(mix_out * new, axis=0, keepdims=True)
        return carry

    lax.fori_loop(0, rows, update, 0, unroll=4)
    state_out = local(state, state_hbm)
    readout = read_buf[...] + skip_ref[...] * inner_wide
    gated = (readout * (gate_in * jax.nn.sigmoid(gate_in))).astype(BF16)

    for copy in mixer_in:
        copy.wait()
    arrivals = []
    for d in range(zeds):
        z = lax.rem(zed + d + 1, zeds)
        mix_send[d] = jnp.dot(
            gated,
            w_share[:chn, pl.ds(pl.multiple_of(z * width, width), width)],
            preferred_element_type=F32,
        ).astype(BF16)
        arrivals.append(remote(mix_send.at[d], mix_recv.at[d], chan=partner))
    crossing = []
    for d in range(zeds):
        z = lax.rem(zed + d + 1, zeds)
        mine = jnp.dot(
            gated,
            w_share[chn : 2 * chn, pl.ds(pl.multiple_of(z * width, width), width)],
            preferred_element_type=F32,
        )
        arrivals[d].wait_recv()
        mine = mine + mix_recv[d].astype(F32)
        if d < zeds - 1:
            mid_send[d] = mine.astype(BF16)
            crossing.append(remote(mid_send.at[d], mid_recv.at[d], chan=2 * z + core))
    share_in = [
        local(
            down_hbm.at[0, :, columns(z, False)],
            w_share.at[pl.ds(0, hid), pl.ds(z * width, width)],
        )
        for z in range(zeds)
    ]
    mid = residual_ref[...].astype(F32) + mine
    for d in range(zeds - 1):
        crossing[d].wait_recv()
        mid = mid + mid_recv[d].astype(F32)

    own_rows = pl.ds(pl.multiple_of(grp * rows, rows), rows)

    def cell(z):
        return rows_x.at[0, own_rows, pl.ds(pl.multiple_of(z * width, width), width)]

    rows_x[0, own_rows, pl.ds(pl.multiple_of(zed * width, width), width)] = mid.astype(BF16)
    over_z = []
    for d in range(1, zeds):
        to = lax.rem(zed + d, zeds)
        over_z.append(remote(cell(zed), cell(zed), chan=2 * to + core))
    over_grp = []
    for d in range(zeds):
        if d:
            over_z[d - 1].wait_recv()
        z = lax.rem(zed + zeds - d, zeds)
        for e in range(1, groups):
            over_grp.append(remote(cell(z), cell(z), grp=lax.rem(grp + e, groups)))
        if d == 0:
            lane = lax.broadcasted_iota(jnp.int32, (rows, 128), 1)
            squares = jnp.sum(mid * mid, axis=1, keepdims=True)
            scores = jnp.dot(
                mid,
                router_ref[...],
                precision=lax.Precision.HIGHEST,
                preferred_element_type=F32,
            )
            stat_own[...] = jnp.where(lane == experts, squares, scores)
            stats = []
            for c in range(1, chans):
                to = lax.rem(me + c, chans)
                stats.append(remote(stat_own, stat_recv.at[c], chan=to))
    summary = stat_own[...]
    for c in range(1, chans):
        stats[c - 1].wait_recv()
        summary = summary + stat_recv[c]
    stat_all[own_rows, :] = summary
    stats = []
    for e in range(1, groups):
        stats.append(
            remote(
                stat_all.at[own_rows, :],
                stat_all.at[own_rows, :],
                grp=lax.rem(grp + e, groups),
            )
        )
    for copy in over_grp:
        copy.wait_recv()
    across = remote(rows_x.at[0], rows_x.at[1], chan=partner)

    tile = min(256, hid)
    for copy in expert_in[0]:
        copy.wait()

    def first(n, carry):
        at = pl.ds(pl.multiple_of(n * tile, tile), tile)
        acc_gate[:, at] = jnp.dot(rows_x[0], w_gate[0, :, at], preferred_element_type=F32)
        acc_up[:, at] = jnp.dot(rows_x[0], w_up[0, :, at], preferred_element_type=F32)
        return carry

    lax.fori_loop(0, hid // tile, first, 0)

    scale = lax.rsqrt(summary[:, experts : experts + 1] / full + EPSILON)
    logits = summary * scale
    first_id, second_id = ids_ref[:, 0:1], ids_ref[:, 1:2]
    chosen_first = jnp.sum(jnp.where(lane == first_id, logits, 0.0), axis=1, keepdims=True)
    chosen_second = jnp.sum(jnp.where(lane == second_id, logits, 0.0), axis=1, keepdims=True)
    weight_first = jax.nn.sigmoid(chosen_first - chosen_second)
    weight_second = 1.0 - weight_first

    for copy in stats:
        copy.wait_recv()
    inv_rms = lax.rsqrt(stat_all[:, experts : experts + 1] / full + EPSILON)
    for copy in expert_in[1]:
        copy.wait()
    across.wait_recv()

    def second(n, carry):
        at = pl.ds(pl.multiple_of(n * tile, tile), tile)
        gate = acc_gate[:, at] + jnp.dot(
            rows_x[1], w_gate[1, :, at], preferred_element_type=F32
        )
        up = acc_up[:, at] + jnp.dot(rows_x[1], w_up[1, :, at], preferred_element_type=F32)
        gate, up = gate * inv_rms, up * inv_rms
        hidden[:, at] = (gate * jax.nn.sigmoid(gate) * up).astype(BF16)
        return carry

    lax.fori_loop(0, hid // tile, second, 0)

    for copy in down_in:
        copy.wait()
    pairs = []
    for d in range(zeds):
        z = lax.rem(zed + d + 1, zeds)
        pair_send[d] = jnp.dot(
            hidden[...],
            w_down[:, pl.ds(pl.multiple_of(z * width, width), width)],
            preferred_element_type=F32,
        ).astype(BF16)
        pairs.append(remote(pair_send.at[d], pair_recv.at[d], chan=partner))
    for copy in share_in:
        copy.wait()
    answers = []
    for d in range(zeds):
        z = lax.rem(zed + d + 1, zeds)
        mine = jnp.dot(
            hidden[...],
            w_share[:hid, pl.ds(pl.multiple_of(z * width, width), width)],
            preferred_element_type=F32,
        )
        pairs[d].wait_recv()
        ans_send[d] = (mine + pair_recv[d].astype(F32)).astype(BF16)
        back = []
        for e in range(1, groups):
            to = lax.rem(grp + e, groups)
            back.append(
                remote(
                    ans_send.at[d, pl.ds(pl.multiple_of(to * rows, rows), rows), :],
                    ans_recv.at[d, grp],
                    grp=to,
                )
            )
        ans_recv[d, grp] = ans_send[d, own_rows, :]
        answers.append(back)
    finals = []
    for d in range(zeds):
        z = lax.rem(zed + d + 1, zeds)
        for copy in answers[d]:
            copy.wait_recv()
        mixed = jnp.zeros((rows, width), F32)
        for w in range(groups):
            label = w // sharers
            coefficient = jnp.where(first_id == label, weight_first, 0.0) + jnp.where(
                second_id == label, weight_second, 0.0
            )
            mixed = mixed + coefficient * ans_recv[d, w].astype(F32)
        if d < zeds - 1:
            fin_send[d] = mixed.astype(BF16)
            finals.append(remote(fin_send.at[d], fin_recv.at[d], chan=2 * z + core))
    out = mid + mixed
    for d in range(zeds - 1):
        finals[d].wait_recv()
        out = out + fin_recv[d].astype(F32)
    layer_ref[...] = out.astype(BF16)
    for copy in sent:
        copy.wait_send()
    state_out.wait()


def per_device(
    residual,
    conv_input,
    gate_input,
    conv_state,
    conv_weight,
    conv_bias,
    state_proj,
    step_proj,
    step_bias,
    decay_rate,
    skip_gain,
    ssm_state,
    out_proj,
    router,
    expert_ids,
    expert_gate,
    expert_up,
    expert_down,
):
    rows, width = residual.shape
    groups = lax.axis_size("grp")
    chans = lax.axis_size("chan")
    zeds = chans // 2
    full = width * chans
    half = full // 2
    chn = conv_input.shape[1]
    hid = expert_gate.shape[2]
    experts = router.shape[1]
    rn = rows // chans
    allrows = rows * groups
    window = conv_state.astype(F32)
    convolved = (
        conv_weight[0] * window[:, 0]
        + conv_weight[1] * window[:, 1]
        + conv_weight[2] * window[:, 2]
        + conv_weight[3] * conv_input.astype(F32)
        + conv_bias
    )
    inner_act = jax.nn.silu(convolved).astype(BF16)
    router_wide = jnp.pad(router.astype(F32), ((0, 0), (0, 128 - experts)))
    padded = -(-state_proj.shape[1] // 128) * 128
    remotes = (
        2 * (chans - 1)
        + zeds
        + 2 * (zeds - 1)
        + zeds * (groups - 1)
        + (chans - 1)
        + (groups - 1)
        + 1
        + zeds
        + zeds * (groups - 1)
        + (zeds - 1)
    )
    locals_ = 2 + 8 * zeds
    scratch = [
        pltpu.VMEM((2, half, hid), BF16),
        pltpu.VMEM((2, half, hid), BF16),
        pltpu.VMEM((hid, half), BF16),
        pltpu.VMEM((max(2 * chn, hid), half), BF16),
        pltpu.VMEM(ssm_state.shape, F32),
        pltpu.VMEM((rows, padded), F32),
        pltpu.VMEM((chans, rn, padded), F32),
        pltpu.VMEM((chans, rn, padded), F32),
        pltpu.VMEM((chans, rn, padded), F32),
        pltpu.VMEM((rows, padded), F32),
        pltpu.VMEM((rows, chn), F32),
        pltpu.VMEM((rows, chn), F32),
        pltpu.VMEM((rows, chn), F32),
        pltpu.VMEM((zeds, rows, width), BF16),
        pltpu.VMEM((zeds, rows, width), BF16),
        pltpu.VMEM((zeds, rows, width), BF16),
        pltpu.VMEM((zeds, rows, width), BF16),
        pltpu.VMEM((2, allrows, half), BF16),
        pltpu.VMEM((rows, 128), F32),
        pltpu.VMEM((chans, rows, 128), F32),
        pltpu.VMEM((allrows, 128), F32),
        pltpu.VMEM((allrows, hid), F32),
        pltpu.VMEM((allrows, hid), F32),
        pltpu.VMEM((allrows, hid), BF16),
        pltpu.VMEM((zeds, allrows, width), BF16),
        pltpu.VMEM((zeds, allrows, width), BF16),
        pltpu.VMEM((zeds, allrows, width), BF16),
        pltpu.VMEM((zeds, groups, rows, width), BF16),
        pltpu.VMEM((zeds, rows, width), BF16),
        pltpu.VMEM((zeds, rows, width), BF16),
        pltpu.SemaphoreType.DMA((locals_,)),
        pltpu.SemaphoreType.DMA((remotes,)),
        pltpu.SemaphoreType.DMA((remotes,)),
    ]
    vmem = pl.BlockSpec(memory_space=pltpu.VMEM)
    anywhere = pl.BlockSpec(memory_space=pl.ANY)
    layer_out, new_state = pl.pallas_call(
        functools.partial(fused, chans, groups, experts),
        out_shape=(
            jax.ShapeDtypeStruct((rows, width), BF16),
            jax.ShapeDtypeStruct(ssm_state.shape, F32),
        ),
        in_specs=[vmem] * 10 + [anywhere] * 5,
        out_specs=(vmem, anywhere),
        scratch_shapes=scratch,
        compiler_params=pltpu.CompilerParams(
            collective_id=0,
            has_side_effects=True,
            vmem_limit_bytes=63 * 2**20,
        ),
        cost_estimate=pl.CostEstimate(
            flops=6 * allrows * full * hid,
            bytes_accessed=6 * full * hid,
            transcendentals=ssm_state.size,
        ),
    )(
        inner_act,
        residual,
        gate_input,
        state_proj,
        step_proj,
        step_bias.reshape(1, chn),
        decay_rate,
        skip_gain.reshape(1, chn),
        router_wide,
        expert_ids,
        ssm_state,
        out_proj,
        expert_gate,
        expert_up,
        expert_down,
    )
    return (layer_out, new_state)


def solution(mesh):
    return jax.shard_map(
        per_device,
        mesh=mesh,
        in_specs=(
            P("grp", "chan"),
            P("grp", "chan"),
            P("grp", "chan"),
            P("grp", None, "chan"),
            P(None, "chan"),
            P("chan"),
            P("chan", None),
            P(None, "chan"),
            P("chan"),
            P(None, "chan"),
            P("chan"),
            P("grp", None, "chan"),
            P("chan", None),
            P("chan", None),
            P("grp", None),
            P("grp", None, "chan"),
            P("grp", None, "chan"),
            P("grp", "chan", None),
        ),
        out_specs=(P("grp", "chan"), P("grp", None, "chan")),
        check_vma=False,
    )
```

```python
import functools

import jax
import jax.numpy as jnp
from jax import lax
from jax.experimental import pallas as pl
from jax.experimental.pallas import tpu as pltpu
from jax.sharding import PartitionSpec as P

EPSILON = 1e-06
F32 = jnp.float32
BF16 = jnp.bfloat16


def fused(
    chans,
    groups,
    experts,
    conv_input_ref,
    conv_state_ref,
    conv_weight_ref,
    conv_bias_ref,
    residual_ref,
    gate_in_ref,
    state_proj_ref,
    step_proj_ref,
    step_bias_ref,
    decay_ref,
    skip_ref,
    router_ref,
    ids_ref,
    ssm_hbm,
    out_proj_hbm,
    gate_hbm,
    up_hbm,
    down_hbm,
    layer_ref,
    state_hbm,
    w_gate,
    w_up,
    w_down,
    w_share,
    state,
    partial,
    proj_send,
    proj_recv,
    proj_all,
    proj,
    step_buf,
    drive_buf,
    read_buf,
    mix_send,
    mix_recv,
    mid_send,
    mid_recv,
    rows_x,
    stat_own,
    stat_recv,
    stat_all,
    acc_gate,
    acc_up,
    hidden,
    pair_send,
    pair_recv,
    ans_send,
    ans_recv,
    fin_send,
    fin_recv,
    local_sem,
    send_sem,
    recv_sem,
):
    me = lax.axis_index("chan")
    grp = lax.axis_index("grp")
    core = lax.rem(me, 2)
    zed = lax.div(me, 2)
    zeds = chans // 2
    partner = me + 1 - 2 * core
    sharers = groups // experts
    rows, width = residual_ref.shape
    full = width * chans
    half = full // 2
    chn = conv_input_ref.shape[1]
    rank = step_proj_ref.shape[0]
    nst = decay_ref.shape[0]
    hid = w_down.shape[0]
    rn = rows // chans
    allrows = rows * groups

    counters = {"local": 0, "remote": 0}

    def local(src, dst):
        k = counters["local"]
        counters["local"] += 1
        copy = pltpu.make_async_copy(src, dst, local_sem.at[k])
        copy.start()
        return copy

    def remote(src, dst, **to):
        k = counters["remote"]
        counters["remote"] += 1
        copy = pltpu.make_async_remote_copy(
            src_ref=src,
            dst_ref=dst,
            send_sem=send_sem.at[k],
            recv_sem=recv_sem.at[k],
            device_id=to,
            device_id_type=pl.DeviceIdType.MESH,
        )
        copy.start()
        sent.append(copy)
        return copy

    sent = []

    def columns(z, other):
        parity = (1 - core) if other else core
        return pl.ds(pl.multiple_of((2 * z + parity) * width, width), width)

    barrier = pltpu.get_barrier_semaphore()
    for d in range(1, chans):
        pl.semaphore_signal(
            barrier,
            inc=1,
            device_id={"chan": lax.rem(me + d, chans)},
            device_id_type=pl.DeviceIdType.MESH,
        )
    for d in range(1, groups):
        pl.semaphore_signal(
            barrier,
            inc=1,
            device_id={"grp": lax.rem(grp + d, groups)},
            device_id_type=pl.DeviceIdType.MESH,
        )

    state_in = local(ssm_hbm, state)

    convolved = (
        conv_weight_ref[0:1, :] * conv_state_ref[0].astype(F32)
        + conv_weight_ref[1:2, :] * conv_state_ref[1].astype(F32)
        + conv_weight_ref[2:3, :] * conv_state_ref[2].astype(F32)
        + conv_weight_ref[3:4, :] * conv_input_ref[...].astype(F32)
        + conv_bias_ref[...]
    )
    inner = (convolved * jax.nn.sigmoid(convolved)).astype(BF16)
    padded = proj.shape[1]
    partial[:, rank:] = jnp.zeros((rows, padded - rank), F32)
    partial[:, : rank + 2 * nst] = lax.dot_general(
        inner, state_proj_ref[...], (((1,), (1,)), ((), ())), preferred_element_type=F32
    )
    for j in range(chans):
        proj_send[j] = partial[j * rn : (j + 1) * rn, :]
    pl.semaphore_wait(barrier, chans - 1 + groups - 1)
    arrivals = []
    for d in range(1, chans):
        to = lax.rem(me + d, chans)
        arrivals.append(remote(proj_send.at[to], proj_recv.at[d], chan=to))
    mixer_in = [
        local(
            out_proj_hbm.at[:, columns(z, p == 0)],
            w_share.at[pl.ds(p * chn, chn), pl.ds(z * width, width)],
        )
        for p in range(2)
        for z in range(zeds)
    ]
    expert_in = [[], []]
    for p in range(2):
        for src, dst in ((gate_hbm, w_gate), (up_hbm, w_up)):
            for z in range(zeds):
                expert_in[p].append(
                    local(
                        src.at[0, columns(z, p == 1), :],
                        dst.at[p, pl.ds(z * width, width), :],
                    )
                )
    down_in = [
        local(down_hbm.at[0, :, columns(z, True)], w_down.at[:, pl.ds(z * width, width)])
        for z in range(zeds)
    ]
    total = proj_send[me]
    for d in range(1, chans):
        arrivals[d - 1].wait_recv()
        total = total + proj_recv[d]
    proj_all[me] = total
    arrivals = []
    for d in range(1, chans):
        to = lax.rem(me + d, chans)
        arrivals.append(remote(proj_all.at[me], proj_all.at[me], chan=to))
    inner_wide = inner.astype(F32)
    router_wide = jnp.concatenate(
        [router_ref[...].astype(F32), jnp.zeros((128 - experts, width), F32)], axis=0
    )
    ids = jnp.concatenate([ids_ref[...].astype(F32), jnp.zeros((126, rows), F32)], axis=0).T
    first_id, second_id = ids[:, 0:1].astype(jnp.int32), ids[:, 1:2].astype(jnp.int32)
    gate_in = gate_in_ref[...].astype(F32)
    for copy in arrivals:
        copy.wait_recv()
    for j in range(chans):
        proj[j * rn : (j + 1) * rn, :] = proj_all[j]

    step_raw = proj[:, :rank]
    step_norm = (
        step_raw * lax.rsqrt(jnp.mean(step_raw * step_raw, axis=1, keepdims=True) + EPSILON)
    ).astype(BF16)
    logit = jnp.dot(step_norm, step_proj_ref[...], preferred_element_type=F32) + step_bias_ref[...]
    step = jnp.maximum(logit, 0.0) + jnp.log1p(jnp.exp(-jnp.abs(logit)))
    step_buf[...] = step
    drive_buf[...] = step * inner_wide
    mixing = proj[:, rank:].T
    in_mix, out_mix = mixing[:nst], mixing[nst : 2 * nst]
    request = lax.broadcasted_iota(jnp.int32, (nst, rows), 1)
    state_in.wait()

    def update(r, carry):
        mine = request == r
        mix_in = jnp.sum(jnp.where(mine, in_mix, 0.0), axis=1, keepdims=True)
        mix_out = jnp.sum(jnp.where(mine, out_mix, 0.0), axis=1, keepdims=True)
        row = pl.ds(r, 1)
        new = jnp.exp(-step_buf[row, :] * decay_ref[...]) * state[r] + drive_buf[row, :] * mix_in
        state[r] = new
        read_buf[row, :] = jnp.sum(mix_out * new, axis=0, keepdims=True)
        return carry

    lax.fori_loop(0, rows, update, 0, unroll=4)
    state_out = local(state, state_hbm)
    readout = read_buf[...] + skip_ref[...] * inner_wide
    gated = (readout * (gate_in * jax.nn.sigmoid(gate_in))).astype(BF16)

    for copy in mixer_in:
        copy.wait()
    arrivals = []
    for d in range(zeds):
        z = lax.rem(zed + d + 1, zeds)
        mix_send[d] = jnp.dot(
            gated,
            w_share[:chn, pl.ds(pl.multiple_of(z * width, width), width)],
            preferred_element_type=F32,
        ).astype(BF16)
        arrivals.append(remote(mix_send.at[d], mix_recv.at[d], chan=partner))
    crossing = []
    for d in range(zeds):
        z = lax.rem(zed + d + 1, zeds)
        mine = jnp.dot(
            gated,
            w_share[chn : 2 * chn, pl.ds(pl.multiple_of(z * width, width), width)],
            preferred_element_type=F32,
        )
        arrivals[d].wait_recv()
        mine = mine + mix_recv[d].astype(F32)
        if d < zeds - 1:
            mid_send[d] = mine.astype(BF16)
            crossing.append(remote(mid_send.at[d], mid_recv.at[d], chan=2 * z + core))
    share_in = [
        local(
            down_hbm.at[0, :, columns(z, False)],
            w_share.at[pl.ds(0, hid), pl.ds(z * width, width)],
        )
        for z in range(zeds)
    ]
    mid = residual_ref[...].astype(F32) + mine
    for d in range(zeds - 1):
        crossing[d].wait_recv()
        mid = mid + mid_recv[d].astype(F32)

    own_rows = pl.ds(pl.multiple_of(grp * rows, rows), rows)

    def cell(z):
        return rows_x.at[0, own_rows, pl.ds(pl.multiple_of(z * width, width), width)]

    rows_x[0, own_rows, pl.ds(pl.multiple_of(zed * width, width), width)] = mid.astype(BF16)
    over_z = []
    for d in range(1, zeds):
        to = lax.rem(zed + d, zeds)
        over_z.append(remote(cell(zed), cell(zed), chan=2 * to + core))
    over_grp = []
    for d in range(zeds):
        if d:
            over_z[d - 1].wait_recv()
        z = lax.rem(zed + zeds - d, zeds)
        over_grp.append(
            [remote(cell(z), cell(z), grp=lax.rem(grp + e, groups)) for e in range(1, groups)]
        )
        if d == 0:
            lane = lax.broadcasted_iota(jnp.int32, (rows, 128), 1)
            squares = jnp.sum(mid * mid, axis=1, keepdims=True)
            scores = lax.dot_general(
                mid,
                router_wide,
                (((1,), (1,)), ((), ())),
                precision=lax.Precision.HIGHEST,
                preferred_element_type=F32,
            )
            stat_own[...] = jnp.where(lane == experts, squares, scores)
            stats = []
            for c in range(1, chans):
                to = lax.rem(me + c, chans)
                stats.append(remote(stat_own, stat_recv.at[c], chan=to))

    tile = min(1024, hid)
    for copy in expert_in[0]:
        copy.wait()
    across = []

    def own_half(d):
        z = lax.rem(zed + zeds - d, zeds)
        part = pl.ds(pl.multiple_of(z * width, width), width)
        for copy in over_grp[d]:
            copy.wait_recv()
        across.append(
            remote(rows_x.at[0, :, part], rows_x.at[1, :, part], chan=partner)
        )

        def first(n, carry):
            at = pl.ds(pl.multiple_of(n * tile, tile), tile)
            gate = jnp.dot(rows_x[0, :, part], w_gate[0, part, at], preferred_element_type=F32)
            up = jnp.dot(rows_x[0, :, part], w_up[0, part, at], preferred_element_type=F32)
            if d:
                gate, up = gate + acc_gate[:, at], up + acc_up[:, at]
            acc_gate[:, at] = gate
            acc_up[:, at] = up
            return carry

        lax.fori_loop(0, hid // tile, first, 0)

    for d in range(zeds // 2):
        own_half(d)
    summary = stat_own[...]
    for c in range(1, chans):
        stats[c - 1].wait_recv()
        summary = summary + stat_recv[c]
    stat_all[own_rows, :] = summary
    stats = []
    for e in range(1, groups):
        stats.append(
            remote(
                stat_all.at[own_rows, :],
                stat_all.at[own_rows, :],
                grp=lax.rem(grp + e, groups),
            )
        )
    for d in range(zeds // 2, zeds):
        own_half(d)

    scale = lax.rsqrt(summary[:, experts : experts + 1] / full + EPSILON)
    logits = summary * scale
    chosen_first = jnp.sum(jnp.where(lane == first_id, logits, 0.0), axis=1, keepdims=True)
    chosen_second = jnp.sum(jnp.where(lane == second_id, logits, 0.0), axis=1, keepdims=True)
    weight_first = jax.nn.sigmoid(chosen_first - chosen_second)
    weight_second = 1.0 - weight_first

    for copy in stats:
        copy.wait_recv()
    inv_rms = lax.rsqrt(stat_all[:, experts : experts + 1] / full + EPSILON)
    for copy in expert_in[1]:
        copy.wait()
    for copy in across:
        copy.wait_recv()

    def second(n, carry):
        at = pl.ds(pl.multiple_of(n * tile, tile), tile)
        gate = acc_gate[:, at] + jnp.dot(
            rows_x[1], w_gate[1, :, at], preferred_element_type=F32
        )
        up = acc_up[:, at] + jnp.dot(rows_x[1], w_up[1, :, at], preferred_element_type=F32)
        gate, up = gate * inv_rms, up * inv_rms
        hidden[:, at] = (gate * jax.nn.sigmoid(gate) * up).astype(BF16)
        return carry

    lax.fori_loop(0, hid // tile, second, 0)

    for copy in down_in:
        copy.wait()
    pairs = []

    def other_half(d):
        z = lax.rem(zed + d + 1, zeds)
        pair_send[d] = jnp.dot(
            hidden[...],
            w_down[:, pl.ds(pl.multiple_of(z * width, width), width)],
            preferred_element_type=F32,
        ).astype(BF16)
        pairs.append(remote(pair_send.at[d], pair_recv.at[d], chan=partner))

    other_half(0)
    for copy in share_in:
        copy.wait()
    answers = []
    for d in range(zeds):
        if d < zeds - 1:
            other_half(d + 1)
        z = lax.rem(zed + d + 1, zeds)
        mine = jnp.dot(
            hidden[...],
            w_share[:hid, pl.ds(pl.multiple_of(z * width, width), width)],
            preferred_element_type=F32,
        )
        pairs[d].wait_recv()
        ans_send[d] = (mine + pair_recv[d].astype(F32)).astype(BF16)
        back = []
        for e in range(1, groups):
            to = lax.rem(grp + e, groups)
            back.append(
                remote(
                    ans_send.at[d, pl.ds(pl.multiple_of(to * rows, rows), rows), :],
                    ans_recv.at[d, grp],
                    grp=to,
                )
            )
        ans_recv[d, grp] = ans_send[d, own_rows, :]
        answers.append(back)
    finals = []
    for d in range(zeds):
        z = lax.rem(zed + d + 1, zeds)
        for copy in answers[d]:
            copy.wait_recv()
        mixed = jnp.zeros((rows, width), F32)
        for w in range(groups):
            label = w // sharers
            coefficient = jnp.where(first_id == label, weight_first, 0.0) + jnp.where(
                second_id == label, weight_second, 0.0
            )
            mixed = mixed + coefficient * ans_recv[d, w].astype(F32)
        if d < zeds - 1:
            fin_send[d] = mixed.astype(BF16)
            finals.append(remote(fin_send.at[d], fin_recv.at[d], chan=2 * z + core))
    out = mid + mixed
    for d in range(zeds - 1):
        finals[d].wait_recv()
        out = out + fin_recv[d].astype(F32)
    layer_ref[...] = out.astype(BF16)
    for copy in sent:
        copy.wait_send()
    state_out.wait()


def deliver(layer_in, state_in, layer_out, state_out, layer_buf, state_buf, in_sem, out_sem):
    parts = in_sem.shape[0] - 1
    count = state_buf.shape[0] // parts
    pieces = [
        (state_in.at[at], state_buf.at[at], state_out.at[at])
        for at in [pl.ds(p * count, count) for p in range(parts)]
    ]
    pieces.append((layer_in, layer_buf, layer_out))
    incoming = [
        pltpu.make_async_copy(src, buf, in_sem.at[k]) for k, (src, buf, _) in enumerate(pieces)
    ]
    outgoing = [
        pltpu.make_async_copy(buf, dst, out_sem.at[k]) for k, (_, buf, dst) in enumerate(pieces)
    ]
    for copy in incoming:
        copy.start()
    for arrived, leaving in zip(incoming, outgoing):
        arrived.wait()
        leaving.start()
    for copy in outgoing:
        copy.wait()


def per_device(
    residual,
    conv_input,
    gate_input,
    conv_state,
    conv_weight,
    conv_bias,
    state_proj,
    step_proj,
    step_bias,
    decay_rate,
    skip_gain,
    ssm_state,
    out_proj,
    router,
    expert_ids,
    expert_gate,
    expert_up,
    expert_down,
):
    rows, width = residual.shape
    groups = lax.axis_size("grp")
    chans = lax.axis_size("chan")
    zeds = chans // 2
    full = width * chans
    half = full // 2
    chn = conv_input.shape[1]
    hid = expert_gate.shape[2]
    experts = router.shape[1]
    rn = rows // chans
    allrows = rows * groups
    padded = -(-state_proj.shape[1] // 128) * 128
    remotes = (
        2 * (chans - 1)
        + zeds
        + 2 * (zeds - 1)
        + zeds * (groups - 1)
        + (chans - 1)
        + (groups - 1)
        + zeds
        + zeds
        + zeds * (groups - 1)
        + (zeds - 1)
    )
    locals_ = 2 + 8 * zeds
    scratch = [
        pltpu.VMEM((2, half, hid), BF16),
        pltpu.VMEM((2, half, hid), BF16),
        pltpu.VMEM((hid, half), BF16),
        pltpu.VMEM((max(2 * chn, hid), half), BF16),
        pltpu.VMEM(ssm_state.shape, F32),
        pltpu.VMEM((rows, padded), F32),
        pltpu.VMEM((chans, rn, padded), F32),
        pltpu.VMEM((chans, rn, padded), F32),
        pltpu.VMEM((chans, rn, padded), F32),
        pltpu.VMEM((rows, padded), F32),
        pltpu.VMEM((rows, chn), F32),
        pltpu.VMEM((rows, chn), F32),
        pltpu.VMEM((rows, chn), F32),
        pltpu.VMEM((zeds, rows, width), BF16),
        pltpu.VMEM((zeds, rows, width), BF16),
        pltpu.VMEM((zeds, rows, width), BF16),
        pltpu.VMEM((zeds, rows, width), BF16),
        pltpu.VMEM((2, allrows, half), BF16),
        pltpu.VMEM((rows, 128), F32),
        pltpu.VMEM((chans, rows, 128), F32),
        pltpu.VMEM((allrows, 128), F32),
        pltpu.VMEM((allrows, hid), F32),
        pltpu.VMEM((allrows, hid), F32),
        pltpu.VMEM((allrows, hid), BF16),
        pltpu.VMEM((zeds, allrows, width), BF16),
        pltpu.VMEM((zeds, allrows, width), BF16),
        pltpu.VMEM((zeds, allrows, width), BF16),
        pltpu.VMEM((zeds, groups, rows, width), BF16),
        pltpu.VMEM((zeds, rows, width), BF16),
        pltpu.VMEM((zeds, rows, width), BF16),
        pltpu.SemaphoreType.DMA((locals_,)),
        pltpu.SemaphoreType.DMA((remotes,)),
        pltpu.SemaphoreType.DMA((remotes,)),
    ]
    vmem = pl.BlockSpec(memory_space=pltpu.VMEM)
    anywhere = pl.BlockSpec(memory_space=pl.ANY)
    layer_out, new_state = pl.pallas_call(
        functools.partial(fused, chans, groups, experts),
        out_shape=(
            jax.ShapeDtypeStruct((rows, width), BF16),
            jax.ShapeDtypeStruct(ssm_state.shape, F32),
        ),
        in_specs=[vmem] * 13 + [anywhere] * 5,
        out_specs=(vmem, anywhere),
        scratch_shapes=scratch,
        compiler_params=pltpu.CompilerParams(
            collective_id=0,
            has_side_effects=True,
            vmem_limit_bytes=63 * 2**20,
        ),
        cost_estimate=pl.CostEstimate(
            flops=6 * allrows * full * hid,
            bytes_accessed=6 * full * hid,
            transcendentals=ssm_state.size,
        ),
    )(
        conv_input,
        conv_state.transpose(1, 0, 2),
        conv_weight,
        conv_bias.reshape(1, chn),
        residual,
        gate_input,
        state_proj.T,
        step_proj,
        step_bias.reshape(1, chn),
        decay_rate,
        skip_gain.reshape(1, chn),
        router.T,
        expert_ids.T,
        ssm_state,
        out_proj,
        expert_gate,
        expert_up,
        expert_down,
    )
    return tuple(
        pl.pallas_call(
            deliver,
            out_shape=(
                jax.ShapeDtypeStruct((rows, width), BF16),
                jax.ShapeDtypeStruct(ssm_state.shape, F32),
            ),
            in_specs=[anywhere] * 2,
            out_specs=(anywhere, anywhere),
            scratch_shapes=[
                pltpu.VMEM((rows, width), BF16),
                pltpu.VMEM(ssm_state.shape, F32),
                pltpu.SemaphoreType.DMA((9,)),
                pltpu.SemaphoreType.DMA((9,)),
            ],
        )(layer_out, new_state)
    )


def solution(mesh):
    return jax.shard_map(
        per_device,
        mesh=mesh,
        in_specs=(
            P("grp", "chan"),
            P("grp", "chan"),
            P("grp", "chan"),
            P("grp", None, "chan"),
            P(None, "chan"),
            P("chan"),
            P("chan", None),
            P(None, "chan"),
            P("chan"),
            P(None, "chan"),
            P("chan"),
            P("grp", None, "chan"),
            P("chan", None),
            P("chan", None),
            P("grp", None),
            P("grp", None, "chan"),
            P("grp", None, "chan"),
            P("grp", "chan", None),
        ),
        out_specs=(P("grp", "chan"), P("grp", None, "chan")),
        check_vma=False,
    )
```
